32 devices in a mesh: row: 4 (over y, core), col: 8 (over z, x).
Axes of the slice: x: 2, y: 2, z: 4, core: 2. Of those that a mesh axis runs over, the one named last changes fastest.
Arguments:
- tokens: bfloat16 [256, 8192], P('col', 'row'), may hold values from -6 to 6
- gate_weight: bfloat16 [8192, 16384], P('row', 'col'), may hold values from -0.09375 to 0.09375
- up_weight: bfloat16 [8192, 16384], P('row', 'col'), may hold values from -0.09375 to 0.09375
- down_weight: bfloat16 [16384, 8192], P('col', 'row'), may hold values from -0.0625 to 0.0625
- gate_mask: int32 [64, 128], P('row', 'col'), may hold values from 0 to 1, as said below
- up_mask: int32 [64, 128], P('row', 'col'), may hold values from 0 to 1, as said below
- down_mask: int32 [128, 64], P('col', 'row'), may hold values from 0 to 1, as said below
Outputs:
- mixed: bfloat16 [256, 8192], P('col', 'row')
The draws below stay inside these ranges and needn't reach their ends.
Inputs may be any that keep to these rules, and one draw needn't show every extreme that they name: `gate_mask`: each entry is 0 or 1; the share of ones differs from one block column of hidden units to another. `up_mask`: each entry is 0 or 1; the share of ones differs from one block column of hidden units to another. `down_mask`: each entry is 0 or 1; the share of ones differs from one block row of hidden units to another.
All inputs are finite; a program needn't handle non-finite values.
Results may differ from the reference program's by a relative error of at most 0.0049.
Values may be sent and summed in bfloat16 or wider, within the bound.
A program may use at most 128 MiB of HBM per device.

```python
import jax
import jax.numpy as jnp

D = 8192
FF = 16384
BLK = 128
TOKENS = 256
GROUP_W = 2048
N_ROW = 4


def draw_gate_mask(key, part):
    levels = jax.random.randint(jax.random.fold_in(key, 101), (1, FF // BLK), 2, 7)
    picked = jax.random.randint(jax.random.fold_in(key, 102), (D // BLK, FF // BLK), 0, 8)
    return (picked < levels).astype(jnp.int32)


def draw_up_mask(key, part):
    levels = jax.random.randint(jax.random.fold_in(key, 201), (1, FF // BLK), 2, 7)
    picked = jax.random.randint(jax.random.fold_in(key, 202), (D // BLK, FF // BLK), 0, 8)
    return (picked < levels).astype(jnp.int32)


def draw_down_mask(key, part):
    levels = jax.random.randint(jax.random.fold_in(key, 301), (FF // BLK, 1), 2, 7)
    picked = jax.random.randint(jax.random.fold_in(key, 302), (FF // BLK, D // BLK), 0, 8)
    return (picked < levels).astype(jnp.int32)


def level_of(own_key, shape, split, least, high):
    loudness, own = 1.0, jax.random.fold_in(own_key, 6)
    for position, blocks in split:
        steps = jnp.exp(jax.random.uniform(jax.random.fold_in(own, position), (blocks,), jnp.float32, least / len(split), high / len(split)))
        loudness = loudness * jnp.repeat(steps, shape[position] // blocks).reshape([-1 if axis == position else 1 for axis in range(len(shape))])
    return loudness


def centred(rng, dims, width, limit, cuts=(), held_as=jnp.bfloat16):
    array = width * jax.random.normal(rng, dims, jnp.float32)
    if cuts:
        array = array * level_of(rng, dims, cuts, -0.22, 0.18)
    return jnp.clip(array, -limit, limit).astype(held_as)


def setup_inputs(seed: int = 0) -> dict:
    splits = jax.random.split(jax.random.key(seed), 8)
    tokens = centred(splits[0], (TOKENS, D), 1.0, 6.0, ((0, 8), (1, 4)))
    gate_weight = centred(splits[1], (D, FF), (D // 2) ** -0.5, 0.09375, ((0, 4), (1, 8)))
    up_weight = centred(splits[2], (D, FF), (D // 2) ** -0.5, 0.09375, ((0, 4), (1, 8)))
    down_weight = centred(splits[3], (FF, D), (FF // 2) ** -0.5, 0.0625, ((0, 8), (1, 4)))
    gate_mask = draw_gate_mask(jax.random.fold_in(splits[7], 71), 0)
    up_mask = draw_up_mask(jax.random.fold_in(splits[7], 71), 0)
    down_mask = draw_down_mask(jax.random.fold_in(splits[7], 71), 0)
    return {"tokens": tokens, "gate_weight": gate_weight, "up_weight": up_weight, "down_weight": down_weight, "gate_mask": gate_mask, "up_mask": up_mask, "down_mask": down_mask}


def widen(block_mask):
    spread = jnp.repeat(jnp.repeat(block_mask, BLK, axis=0), BLK, axis=1)
    return spread.astype(jnp.bfloat16)


def reference(tokens, gate_weight, up_weight, down_weight, gate_mask, up_mask, down_mask):
    gate_eff = gate_weight * widen(gate_mask)
    up_eff = up_weight * widen(up_mask)
    down_eff = down_weight * widen(down_mask)
    gate = jnp.zeros((TOKENS, FF), jnp.float32)
    up = jnp.zeros((TOKENS, FF), jnp.float32)
    for group in range(N_ROW):
        lower = group * GROUP_W
        columns = tokens[:, lower:lower + GROUP_W]
        gate = gate + jnp.dot(columns, gate_eff[lower:lower + GROUP_W], preferred_element_type=jnp.float32)
        up = up + jnp.dot(columns, up_eff[lower:lower + GROUP_W], preferred_element_type=jnp.float32)
    hidden = (jax.nn.silu(gate) * up).astype(jnp.bfloat16)
    return jnp.dot(hidden, down_eff, preferred_element_type=jnp.float32).astype(jnp.bfloat16)
```

```python
import functools

import jax
import jax.numpy as jnp
from jax import lax
from jax.experimental import pallas as pl
from jax.experimental.pallas import tpu as pltpu
from jax.sharding import PartitionSpec as P

BLK = 128
GROUPS = 2
CHUNKS = 4
OUT_CHUNKS = 2
MESH = pl.DeviceIdType.MESH
F32 = jnp.float32
BF16 = jnp.bfloat16


def flip(a, d):
    bit = 1
    while bit <= d:
        if d & bit:
            a = a + bit - 2 * bit * lax.rem(lax.div(a, bit), 2)
        bit *= 2
    return a


def at_rows(start, size):
    return pl.ds(pl.multiple_of(start, 16), size)


def kernel(
    Y, Z, X,
    tokens, gate_w, up_w, down_w, gate_m, up_m, down_m,
    out,
    tok, wg, wu, wd, part, send1, recv1, send2, recv2, hid, acc,
    send3, recv3, send4, recv4,
    w_sem, own_sem, az_s, az_r, ax_s, ax_r,
    s1, r1, s2, r2, s3, r3, s4, r4, s5, r5, s6, r6,
):
    G, NC, OC = GROUPS, CHUNKS, OUT_CHUNKS
    U = G * NC
    rows = tokens.shape[0] // G
    M = tok.shape[1]
    half = M // 2
    R = half // Y
    hc = wg.shape[2]
    depth = wg.shape[1]
    oc_w = wd.shape[2] // OC
    row, col = lax.axis_index("row"), lax.axis_index("col")
    y, k = lax.div(row, 2), lax.rem(row, 2)
    z, x = lax.div(col, X), lax.rem(col, X)
    sib = (y * 2 + 1 - k, col)

    def y_peer(d):
        return (flip(y, d) * 2 + k, col)

    def z_peer(d):
        return (row, flip(z, d) * X + x)

    def x_peer(e):
        return (row, z * X + flip(x, e))

    def remote(src, dst, send, recv, who):
        return pltpu.make_async_remote_copy(
            src_ref=src, dst_ref=dst, send_sem=send, recv_sem=recv,
            device_id=who, device_id_type=MESH,
        )

    def weight_copies(n):
        cols = pl.ds(n * hc, hc)
        return (
            pltpu.make_async_copy(gate_w.at[:, cols], wg.at[n], w_sem.at[0, n]),
            pltpu.make_async_copy(up_w.at[:, cols], wu.at[n], w_sem.at[1, n]),
        )

    def down_copy(n):
        return pltpu.make_async_copy(
            down_w.at[at_rows(n * hc, hc)], wd.at[n], w_sem.at[2, n]
        )

    def place(xs, zs):
        return at_rows((xs * Z + zs) * rows, rows)

    def own_copy(g):
        return pltpu.make_async_copy(
            tokens.at[pl.ds(g * rows, rows)], tok.at[g, place(x, z)], own_sem.at[g]
        )

    def gather_z(g, d):
        return remote(
            tokens.at[pl.ds(g * rows, rows)], tok.at[g, place(x, z)],
            az_s.at[g, d], az_r.at[g, d], z_peer(d),
        )

    def gather_x(g, d, e):
        there = place(x, flip(z, d))
        src = tokens.at[pl.ds(g * rows, rows)] if d == 0 else tok.at[g, there]
        return remote(src, tok.at[g, there], ax_s.at[g, d, e], ax_r.at[g, d, e], x_peer(e))

    def c1(j):
        return remote(send1.at[j], recv1.at[j], s1.at[j], r1.at[j], sib)

    def c2(j, d):
        return remote(send2.at[j, d - 1], recv2.at[j, d - 1], s2.at[j, d], r2.at[j, d], y_peer(d))

    def c3(j, d):
        ref = hid.at[j, at_rows((k * Y + y) * R, R)]
        return remote(ref, ref, s3.at[j, d], r3.at[j, d], y_peer(d))

    def c4(j, d):
        ref = hid.at[j, at_rows((k * Y + flip(y, d)) * R, R)]
        return remote(ref, ref, s4.at[j, d], r4.at[j, d], sib)

    def c5(g, e, o):
        return remote(
            send3.at[g, o, e - 1], recv3.at[g, o, e - 1],
            s5.at[g, o, e], r5.at[g, o, e], x_peer(e),
        )

    def c6(g, d, o):
        return remote(
            send4.at[g, o, d - 1], recv4.at[g, o, d - 1],
            s6.at[g, o, d], r6.at[g, o, d], z_peer(d),
        )

    def spread(bit):
        return jnp.full((16, BLK), bit.astype(F32), F32).astype(BF16)[None]

    def mask_gate_up(n):
        @pl.loop(0, depth // BLK)
        def _(b):
            band = at_rows(b * BLK, BLK)
            for w_ref, m_ref in ((wg, gate_m), (wu, up_m)):
                for h in range(hc // BLK):
                    cols = pl.ds(h * BLK, BLK)
                    tile = w_ref[n, band, cols].reshape(BLK // 16, 16, BLK)
                    tile = tile * spread(m_ref[b, n * (hc // BLK) + h])
                    w_ref[n, band, cols] = tile.reshape(BLK, BLK)

    def mask_down(n):
        wide = wd.shape[2] // BLK
        for b in range(hc // BLK):
            band = pl.ds(b * BLK, BLK)

            @pl.loop(0, wide)
            def _(h):
                cols = pl.ds(pl.multiple_of(h * BLK, BLK), BLK)
                tile = wd[n, band, cols].reshape(BLK // 16, 16, BLK)
                tile = tile * spread(down_m[n * (hc // BLK) + b, h])
                wd[n, band, cols] = tile.reshape(BLK, BLK)

    for n in range(NC):
        for copy in weight_copies(n):
            copy.start()
    for g in range(G):
        own_copy(g).start()
    barrier = pltpu.get_barrier_semaphore()
    peers = [sib]
    peers += [y_peer(d) for d in range(1, Y)]
    peers += [z_peer(d) for d in range(1, Z)]
    peers += [x_peer(e) for e in range(1, X)]
    for who in peers:
        pl.semaphore_signal(barrier, inc=1, device_id=who, device_id_type=MESH)
    pl.semaphore_wait(barrier, len(peers))

    for g in range(G):
        for d in range(1, Z):
            gather_z(g, d).start()
        for e in range(1, X):
            gather_x(g, 0, e).start()
    for n in range(NC):
        down_copy(n).start()

    def forward(g, d):
        gather_z(g, d).wait_recv()
        for e in range(1, X):
            gather_x(g, d, e).start()

    def tokens_in(g):
        own_copy(g).wait()
        for d in range(Z):
            for e in range(1, X):
                gather_x(g, d, e).wait_recv()

    for n in range(NC):
        for copy in weight_copies(n):
            copy.wait()
        mask_gate_up(n)
        for d in range(1, Z):
            if min(d - 1, NC - 1) == n:
                forward(0, d)
    tokens_in(0)

    def partial_sums(j):
        g, n = lax.div(j, NC), lax.rem(j, NC)
        part[j, :, :hc] = jnp.dot(tok[g], wg[n], preferred_element_type=F32)
        part[j, :, hc:] = jnp.dot(tok[g], wu[n], preferred_element_type=F32)
        send1[j] = part[j, at_rows((1 - k) * half, half)].astype(BF16)
        c1(j).start()

    def chip_sum(j, yy):
        own = part[j, at_rows((k * Y + yy) * R, R)]
        return own + recv1[j, at_rows(yy * R, R)].astype(F32)

    def over_y(j):
        c1(j).wait_recv()
        for d in range(1, Y):
            send2[j, d - 1] = chip_sum(j, flip(y, d)).astype(BF16)
            c2(j, d).start()

    def activate(j):
        total = chip_sum(j, y)
        for d in range(1, Y):
            c2(j, d).wait_recv()
            total += recv2[j, d - 1].astype(F32)
        value, scale = total[:, :hc], total[:, hc:]
        hid[j, at_rows((k * Y + y) * R, R)] = (value / (1.0 + jnp.exp(-value)) * scale).astype(BF16)
        for d in range(1, Y):
            c3(j, d).start()
        c4(j, 0).start()

    def to_sibling(j):
        for d in range(1, Y):
            c3(j, d).wait_recv()
            c4(j, d).start()

    def down(j):
        g, n = lax.div(j, NC), lax.rem(j, NC)
        for d in range(Y):
            c4(j, d).wait_recv()

        for o in range(OC):
            cols = pl.ds(o * oc_w, oc_w)
            term = jnp.dot(hid[j], wd[n, :, cols], preferred_element_type=F32)

            @pl.when(n == 0)
            def _():
                acc[g, :, cols] = term

            @pl.when(n > 0)
            def _():
                acc[g, :, cols] += term

            @pl.when(n == NC - 1)
            def _():
                for e in range(1, X):
                    send3[g, o, e - 1] = acc[
                        g, at_rows(flip(x, e) * Z * rows, Z * rows), cols
                    ].astype(BF16)
                    c5(g, e, o).start()

    def x_sum(g, o, zz):
        total = acc[g, at_rows((x * Z + zz) * rows, rows), o * oc_w:(o + 1) * oc_w]
        for e in range(1, X):
            total += recv3[g, o, e - 1, at_rows(zz * rows, rows)].astype(F32)
        return total

    def over_z(g):
        for o in range(OC):
            for e in range(1, X):
                c5(g, e, o).wait_recv()
            for d in range(1, Z):
                send4[g, o, d - 1] = x_sum(g, o, flip(z, d)).astype(BF16)
                c6(g, d, o).start()

    def finish(g):
        for o in range(OC):
            total = x_sum(g, o, z)
            for d in range(1, Z):
                c6(g, d, o).wait_recv()
                total += recv4[g, o, d - 1].astype(F32)
            out[at_rows(g * rows, rows), o * oc_w:(o + 1) * oc_w] = total.astype(BF16)

    @pl.loop(0, U + 6)
    def _(t):
        for g in range(1, G):
            @pl.when(t == g * NC)
            def _():
                tokens_in(g)

        @pl.when(t < U)
        def _():
            partial_sums(t)

        for g in range(1, G):
            @pl.when(t == (g - 1) * NC)
            def _():
                for d in range(1, Z):
                    forward(g, d)

        for stage, work in ((1, over_y), (2, activate), (3, to_sibling)):
            @pl.when((t >= stage) & (t < U + stage))
            def _():
                work(t - stage)

        @pl.when(t < NC)
        def _():
            down_copy(t).wait()
            mask_down(t)

        @pl.when((t >= 4) & (t < U + 4))
        def _():
            down(t - 4)

        for g in range(G):
            @pl.when(t == (g + 1) * NC + 4)
            def _():
                over_z(g)

            @pl.when(t == (g + 1) * NC + 5)
            def _():
                finish(g)

    @pl.loop(0, U)
    def _(j):
        c1(j).wait_send()
        for d in range(1, Y):
            c2(j, d).wait_send()
            c3(j, d).wait_send()
        for d in range(Y):
            c4(j, d).wait_send()

    for g in range(G):
        for d in range(1, Z):
            gather_z(g, d).wait_send()
        for d in range(Z):
            for e in range(1, X):
                gather_x(g, d, e).wait_send()
        for o in range(OC):
            for e in range(1, X):
                c5(g, e, o).wait_send()
            for d in range(1, Z):
                c6(g, d, o).wait_send()


def on_device(n_row, n_col, tokens, gate_w, up_w, down_w, gate_m, up_m, down_m):
    Y = n_row // 2
    X = 1
    while X * X * 4 <= n_col:
        X *= 2
    Z = n_col // X
    G, NC, OC = GROUPS, CHUNKS, OUT_CHUNKS
    U = G * NC
    t_rows, depth = tokens.shape
    rows = t_rows // G
    M = rows * n_col
    R = M // n_row
    hc = gate_w.shape[1] // NC
    wide = down_w.shape[1]
    ow = wide // OC
    dma = pltpu.SemaphoreType.DMA
    return pl.pallas_call(
        functools.partial(kernel, Y, Z, X),
        out_shape=jax.ShapeDtypeStruct((t_rows, wide), BF16),
        in_specs=[pl.BlockSpec(memory_space=pl.ANY)] * 4
        + [pl.BlockSpec(memory_space=pltpu.SMEM)] * 3,
        out_specs=pl.BlockSpec(memory_space=pltpu.VMEM),
        scratch_shapes=[
            pltpu.VMEM((G, M, depth), BF16),
            pltpu.VMEM((NC, depth, hc), BF16),
            pltpu.VMEM((NC, depth, hc), BF16),
            pltpu.VMEM((NC, hc, wide), BF16),
            pltpu.VMEM((U, M, 2 * hc), F32),
            pltpu.VMEM((U, M // 2, 2 * hc), BF16),
            pltpu.VMEM((U, M // 2, 2 * hc), BF16),
            pltpu.VMEM((U, Y - 1, R, 2 * hc), BF16),
            pltpu.VMEM((U, Y - 1, R, 2 * hc), BF16),
            pltpu.VMEM((U, M, hc), BF16),
            pltpu.VMEM((G, M, wide), F32),
            pltpu.VMEM((G, OC, X - 1, Z * rows, ow), BF16),
            pltpu.VMEM((G, OC, X - 1, Z * rows, ow), BF16),
            pltpu.VMEM((G, OC, Z - 1, rows, ow), BF16),
            pltpu.VMEM((G, OC, Z - 1, rows, ow), BF16),
            dma((3, NC)), dma((G,)),
            dma((G, Z)), dma((G, Z)), dma((G, Z, X)), dma((G, Z, X)),
            dma((U,)), dma((U,)),
            dma((U, Y)), dma((U, Y)),
            dma((U, Y)), dma((U, Y)),
            dma((U, Y)), dma((U, Y)),
            dma((G, OC, X)), dma((G, OC, X)),
            dma((G, OC, Z)), dma((G, OC, Z)),
        ],
        compiler_params=pltpu.CompilerParams(
            collective_id=0, has_side_effects=True, vmem_limit_bytes=56 * 2**20
        ),
    )(tokens, gate_w, up_w, down_w, gate_m, up_m, down_m)


def solution(mesh):
    placed = (
        P("col", "row"),
        P("row", "col"),
        P("row", "col"),
        P("col", "row"),
        P("row", "col"),
        P("row", "col"),
        P("col", "row"),
    )
    body = functools.partial(on_device, mesh.shape["row"], mesh.shape["col"])
    return jax.shard_map(
        body, mesh=mesh, in_specs=placed, out_specs=P("col", "row"), check_vma=False
    )
```

```python
import functools

import jax
import jax.numpy as jnp
from jax import lax
from jax.experimental import pallas as pl
from jax.experimental.pallas import tpu as pltpu
from jax.sharding import PartitionSpec as P

BLK = 128
GROUPS = 2
CHUNKS = 4
OUT_CHUNKS = 4
OVER_Y, ACTIVATE, TO_SIBLING, DOWN, OVER_Z, FINISH = 1, 3, 5, 6, 8, 10
MESH = pl.DeviceIdType.MESH
F32 = jnp.float32
BF16 = jnp.bfloat16


def flip(a, d):
    bit = 1
    while bit <= d:
        if d & bit:
            a = a + bit - 2 * bit * lax.rem(lax.div(a, bit), 2)
        bit *= 2
    return a


def at_rows(start, size):
    return pl.ds(pl.multiple_of(start, 16), size)


def kernel(
    Y, Z, X,
    tokens, gate_w, up_w, down_w, gate_m, up_m, down_m,
    out,
    tok, wg, wu, wd, part, send1, recv1, send2, recv2, hid, acc,
    send3, recv3, send4, recv4,
    w_sem, own_sem, az_s, az_r, ax_s, ax_r,
    s1, r1, s2, r2, s3, r3, s4, r4, s5, r5, s6, r6,
):
    G, NC, OC = GROUPS, CHUNKS, OUT_CHUNKS
    U = G * NC
    rows = tokens.shape[0] // G
    M = tok.shape[1]
    half = M // 2
    R = half // Y
    hc = wg.shape[2]
    depth = wg.shape[1]
    oc_w = wd.shape[2] // OC
    row, col = lax.axis_index("row"), lax.axis_index("col")
    y, k = lax.div(row, 2), lax.rem(row, 2)
    z, x = lax.div(col, X), lax.rem(col, X)
    sib = (y * 2 + 1 - k, col)

    def y_peer(d):
        return (flip(y, d) * 2 + k, col)

    def z_peer(d):
        return (row, flip(z, d) * X + x)

    def x_peer(e):
        return (row, z * X + flip(x, e))

    def remote(src, dst, send, recv, who):
        return pltpu.make_async_remote_copy(
            src_ref=src, dst_ref=dst, send_sem=send, recv_sem=recv,
            device_id=who, device_id_type=MESH,
        )

    def weight_copies(n):
        cols = pl.ds(n * hc, hc)
        return (
            pltpu.make_async_copy(gate_w.at[:, cols], wg.at[n], w_sem.at[0, n]),
            pltpu.make_async_copy(up_w.at[:, cols], wu.at[n], w_sem.at[1, n]),
        )

    def down_copy(n):
        return pltpu.make_async_copy(
            down_w.at[at_rows(n * hc, hc)], wd.at[n], w_sem.at[2, n]
        )

    def place(xs, zs):
        return at_rows((xs * Z + zs) * rows, rows)

    def own_copy(g):
        return pltpu.make_async_copy(
            tokens.at[pl.ds(g * rows, rows)], tok.at[g, place(x, z)], own_sem.at[g]
        )

    def gather_z(g, d):
        return remote(
            tokens.at[pl.ds(g * rows, rows)], tok.at[g, place(x, z)],
            az_s.at[g, d], az_r.at[g, d], z_peer(d),
        )

    def gather_x(g, d, e):
        there = place(x, flip(z, d))
        src = tokens.at[pl.ds(g * rows, rows)] if d == 0 else tok.at[g, there]
        return remote(src, tok.at[g, there], ax_s.at[g, d, e], ax_r.at[g, d, e], x_peer(e))

    def c1(j):
        return remote(send1.at[j], recv1.at[j], s1.at[j], r1.at[j], sib)

    def c2(j, d):
        return remote(send2.at[j, d - 1], recv2.at[j, d - 1], s2.at[j, d], r2.at[j, d], y_peer(d))

    def c3(j, d):
        ref = hid.at[j, at_rows((k * Y + y) * R, R)]
        return remote(ref, ref, s3.at[j, d], r3.at[j, d], y_peer(d))

    def c4(j, d):
        ref = hid.at[j, at_rows((k * Y + flip(y, d)) * R, R)]
        return remote(ref, ref, s4.at[j, d], r4.at[j, d], sib)

    def c5(g, e, o):
        return remote(
            send3.at[g, o, e - 1], recv3.at[g, o, e - 1],
            s5.at[g, o, e], r5.at[g, o, e], x_peer(e),
        )

    def c6(g, d, o):
        return remote(
            send4.at[g, o, d - 1], recv4.at[g, o, d - 1],
            s6.at[g, o, d], r6.at[g, o, d], z_peer(d),
        )

    def spread(bit):
        return jnp.full((16, BLK), bit.astype(F32), F32).astype(BF16)[None]

    def mask_gate_up(n):
        @pl.loop(0, depth // BLK)
        def _(b):
            band = at_rows(b * BLK, BLK)
            for w_ref, m_ref in ((wg, gate_m), (wu, up_m)):
                for h in range(hc // BLK):
                    cols = pl.ds(h * BLK, BLK)
                    tile = w_ref[n, band, cols].reshape(BLK // 16, 16, BLK)
                    tile = tile * spread(m_ref[b, n * (hc // BLK) + h])
                    w_ref[n, band, cols] = tile.reshape(BLK, BLK)

    def mask_down(n):
        wide = wd.shape[2] // BLK
        for b in range(hc // BLK):
            band = pl.ds(b * BLK, BLK)

            @pl.loop(0, wide)
            def _(h):
                cols = pl.ds(pl.multiple_of(h * BLK, BLK), BLK)
                tile = wd[n, band, cols].reshape(BLK // 16, 16, BLK)
                tile = tile * spread(down_m[n * (hc // BLK) + b, h])
                wd[n, band, cols] = tile.reshape(BLK, BLK)

    for n in range(NC):
        for copy in weight_copies(n):
            copy.start()
    for g in range(G):
        own_copy(g).start()
    barrier = pltpu.get_barrier_semaphore()
    peers = [sib]
    peers += [y_peer(d) for d in range(1, Y)]
    peers += [z_peer(d) for d in range(1, Z)]
    peers += [x_peer(e) for e in range(1, X)]
    for who in peers:
        pl.semaphore_signal(barrier, inc=1, device_id=who, device_id_type=MESH)
    pl.semaphore_wait(barrier, len(peers))

    def send_own(g):
        for d in range(1, Z):
            gather_z(g, d).start()
        for e in range(1, X):
            gather_x(g, 0, e).start()

    send_own(0)
    for n in range(NC):
        down_copy(n).start()

    def forward(g, d):
        gather_z(g, d).wait_recv()
        for e in range(1, X):
            gather_x(g, d, e).start()

    def tokens_in(g):
        own_copy(g).wait()
        for d in range(Z):
            for e in range(1, X):
                gather_x(g, d, e).wait_recv()

    for n in range(NC):
        for copy in weight_copies(n):
            copy.wait()
        mask_gate_up(n)
        for d in range(1, Z):
            if min(d - 1, NC - 1) == n:
                forward(0, d)
    for g in range(1, G):
        send_own(g)
    tokens_in(0)

    def partial_sums(j):
        g, n = lax.div(j, NC), lax.rem(j, NC)
        part[j, :, :hc] = jnp.dot(tok[g], wg[n], preferred_element_type=F32)
        part[j, :, hc:] = jnp.dot(tok[g], wu[n], preferred_element_type=F32)
        send1[j] = part[j, at_rows((1 - k) * half, half)].astype(BF16)
        c1(j).start()

    def chip_sum(j, yy):
        own = part[j, at_rows((k * Y + yy) * R, R)]
        return own + recv1[j, at_rows(yy * R, R)].astype(F32)

    def over_y(j):
        c1(j).wait_recv()
        for d in range(1, Y):
            send2[j, d - 1] = chip_sum(j, flip(y, d)).astype(BF16)
            c2(j, d).start()

    def activate(j):
        total = chip_sum(j, y)
        for d in range(1, Y):
            c2(j, d).wait_recv()
            total += recv2[j, d - 1].astype(F32)
        value, scale = total[:, :hc], total[:, hc:]
        hid[j, at_rows((k * Y + y) * R, R)] = (value / (1.0 + jnp.exp(-value)) * scale).astype(BF16)
        for d in range(1, Y):
            c3(j, d).start()
        c4(j, 0).start()

    def to_sibling(j):
        for d in range(1, Y):
            c3(j, d).wait_recv()
            c4(j, d).start()

    def down(j):
        g, n = lax.div(j, NC), lax.rem(j, NC)
        for d in range(Y):
            c4(j, d).wait_recv()

        for o in range(OC):
            cols = pl.ds(o * oc_w, oc_w)
            term = jnp.dot(hid[j], wd[n, :, cols], preferred_element_type=F32)

            @pl.when(n == 0)
            def _():
                acc[g, :, cols] = term

            @pl.when(n > 0)
            def _():
                acc[g, :, cols] += term

            @pl.when(n == NC - 1)
            def _():
                for e in range(1, X):
                    send3[g, o, e - 1] = acc[
                        g, at_rows(flip(x, e) * Z * rows, Z * rows), cols
                    ].astype(BF16)
                    c5(g, e, o).start()

    def x_sum(g, o, zz):
        total = acc[g, at_rows((x * Z + zz) * rows, rows), o * oc_w:(o + 1) * oc_w]
        for e in range(1, X):
            total += recv3[g, o, e - 1, at_rows(zz * rows, rows)].astype(F32)
        return total

    def over_z(g):
        for o in range(OC):
            for e in range(1, X):
                c5(g, e, o).wait_recv()
            for d in range(1, Z):
                send4[g, o, d - 1] = x_sum(g, o, flip(z, d)).astype(BF16)
                c6(g, d, o).start()

    def finish(g):
        for o in range(OC):
            total = x_sum(g, o, z)
            for d in range(1, Z):
                c6(g, d, o).wait_recv()
                total += recv4[g, o, d - 1].astype(F32)
            out[at_rows(g * rows, rows), o * oc_w:(o + 1) * oc_w] = total.astype(BF16)

    @pl.loop(0, U + FINISH)
    def _(t):
        for g in range(1, G):
            @pl.when(t == g * NC)
            def _():
                tokens_in(g)

        @pl.when(t < U)
        def _():
            partial_sums(t)

        for g in range(1, G):
            for d in range(1, Z):
                @pl.when(t == (g - 1) * NC + min(d - 1, NC - 2))
                def _():
                    forward(g, d)

        for stage, work in (
            (OVER_Y, over_y), (ACTIVATE, activate), (TO_SIBLING, to_sibling)
        ):
            @pl.when((t >= stage) & (t < U + stage))
            def _():
                work(t - stage)

        @pl.when(t < NC)
        def _():
            down_copy(t).wait()
            mask_down(t)

        @pl.when((t >= DOWN) & (t < U + DOWN))
        def _():
            down(t - DOWN)

        for g in range(G):
            @pl.when(t == (g + 1) * NC - 1 + OVER_Z)
            def _():
                over_z(g)

            @pl.when(t == (g + 1) * NC - 1 + FINISH)
            def _():
                finish(g)

    @pl.loop(0, U)
    def _(j):
        c1(j).wait_send()
        for d in range(1, Y):
            c2(j, d).wait_send()
            c3(j, d).wait_send()
        for d in range(Y):
            c4(j, d).wait_send()

    for g in range(G):
        for d in range(1, Z):
            gather_z(g, d).wait_send()
        for d in range(Z):
            for e in range(1, X):
                gather_x(g, d, e).wait_send()
        for o in range(OC):
            for e in range(1, X):
                c5(g, e, o).wait_send()
            for d in range(1, Z):
                c6(g, d, o).wait_send()


def on_device(n_row, n_col, tokens, gate_w, up_w, down_w, gate_m, up_m, down_m):
    Y = n_row // 2
    X = 1
    while X * X * 4 <= n_col:
        X *= 2
    Z = n_col // X
    G, NC, OC = GROUPS, CHUNKS, OUT_CHUNKS
    U = G * NC
    t_rows, depth = tokens.shape
    rows = t_rows // G
    M = rows * n_col
    R = M // n_row
    hc = gate_w.shape[1] // NC
    wide = down_w.shape[1]
    ow = wide // OC
    dma = pltpu.SemaphoreType.DMA
    return pl.pallas_call(
        functools.partial(kernel, Y, Z, X),
        out_shape=jax.ShapeDtypeStruct((t_rows, wide), BF16),
        in_specs=[pl.BlockSpec(memory_space=pl.ANY)] * 4
        + [pl.BlockSpec(memory_space=pltpu.SMEM)] * 3,
        out_specs=pl.BlockSpec(memory_space=pltpu.VMEM),
        scratch_shapes=[
            pltpu.VMEM((G, M, depth), BF16),
            pltpu.VMEM((NC, depth, hc), BF16),
            pltpu.VMEM((NC, depth, hc), BF16),
            pltpu.VMEM((NC, hc, wide), BF16),
            pltpu.VMEM((U, M, 2 * hc), F32),
            pltpu.VMEM((U, M // 2, 2 * hc), BF16),
            pltpu.VMEM((U, M // 2, 2 * hc), BF16),
            pltpu.VMEM((U, Y - 1, R, 2 * hc), BF16),
            pltpu.VMEM((U, Y - 1, R, 2 * hc), BF16),
            pltpu.VMEM((U, M, hc), BF16),
            pltpu.VMEM((G, M, wide), F32),
            pltpu.VMEM((G, OC, X - 1, Z * rows, ow), BF16),
            pltpu.VMEM((G, OC, X - 1, Z * rows, ow), BF16),
            pltpu.VMEM((G, OC, Z - 1, rows, ow), BF16),
            pltpu.VMEM((G, OC, Z - 1, rows, ow), BF16),
            dma((3, NC)), dma((G,)),
            dma((G, Z)), dma((G, Z)), dma((G, Z, X)), dma((G, Z, X)),
            dma((U,)), dma((U,)),
            dma((U, Y)), dma((U, Y)),
            dma((U, Y)), dma((U, Y)),
            dma((U, Y)), dma((U, Y)),
            dma((G, OC, X)), dma((G, OC, X)),
            dma((G, OC, Z)), dma((G, OC, Z)),
        ],
        compiler_params=pltpu.CompilerParams(
            collective_id=0, has_side_effects=True, vmem_limit_bytes=56 * 2**20
        ),
    )(tokens, gate_w, up_w, down_w, gate_m, up_m, down_m)


def solution(mesh):
    placed = (
        P("col", "row"),
        P("row", "col"),
        P("row", "col"),
        P("col", "row"),
        P("row", "col"),
        P("row", "col"),
        P("col", "row"),
    )
    body = functools.partial(on_device, mesh.shape["row"], mesh.shape["col"])
    return jax.shard_map(
        body, mesh=mesh, in_specs=placed, out_specs=P("col", "row"), check_vma=False
    )
```
